128 devices in a mesh: gx: 2 (over y_lo), vy: 16 (over z, y_hi, core), vx: 4 (over x).
Axes of the slice: x: 4, y: 4 (y_hi: 2, y_lo: 2; y = y_hi * 2 + y_lo), z: 4, core: 2. Of those that a mesh axis runs over, the one named last changes fastest.
Arguments:
- populations: float32 [32, 32, 32, 2048], P('vy', 'vx', None, 'gx'), may hold values from 0 to 15, as said below
Outputs:
- advanced: float32 [32, 32, 32, 2048], P('vy', 'vx', None, 'gx')
The draws below stay inside these ranges and needn't reach their ends.
Inputs may be any that keep to these rules, and one draw needn't show every extreme that they name: `populations`: every entry is positive.
All inputs are finite; a program needn't handle non-finite values.
Results may differ from the reference program's by a relative error of at most 0.0003.
Values sent between devices are 32-bit elements; how exact they have to be, the bound alone decides.
A program may use at most 64 MiB of HBM per device.

```python
import math
import jax
import jax.numpy as jnp
from jax import lax

NVY = 32
NVX = 32
NY = 32
STEPS = 2
NX = 2048


def draw_populations(key, part):
    keys = jax.random.split(key, 6)
    speeds_y = -4.0 + (jnp.arange(NVY, dtype=jnp.float32) + 0.5) * (8.0 / NVY)
    speeds_x = -4.0 + (jnp.arange(NVX, dtype=jnp.float32) + 0.5) * (8.0 / NVX)
    block_log = jax.random.uniform(keys[2], (NY, NX // 8), jnp.float32, math.log(0.25), math.log(20.0))
    block_width = jnp.repeat(jnp.exp(block_log), 8, axis=1)
    width = block_width * jax.random.uniform(keys[5], (NY, NX), jnp.float32, 0.8, 1.2)
    drift_x = jax.random.uniform(keys[0], (NY, NX), jnp.float32, -0.5, 0.5)
    drift_y = jax.random.uniform(keys[1], (NY, NX), jnp.float32, -0.5, 0.5)
    amplitude = jax.random.uniform(keys[3], (NY, NX), jnp.float32, 0.5, 1.5)
    noise = jax.random.uniform(keys[4], (NVY, NVX, NY, NX), jnp.float32, 0.5, 1.5)
    peculiar_abscissa = speeds_x[None, :, None, None] - drift_x[None, None]
    peculiar_ordinate = speeds_y[:, None, None, None] - drift_y[None, None]
    envelope = jnp.exp(-(peculiar_abscissa * peculiar_abscissa + peculiar_ordinate * peculiar_ordinate) / width[None, None])
    return (amplitude[None, None] * (envelope + 0.02) * noise).astype(jnp.float32)


def setup_inputs(seed: int = 0) -> dict:
    key_of = jax.random.split(jax.random.key(seed), 2)
    return {
        "populations": draw_populations(jax.random.fold_in(key_of[1], 71), 0),
    }


speed_limit = 4.0
marching_delta = 0.125
inverse_relax_period = 16.0
viscous_conductive_ratio = 2.0 / 3.0
thermal_floor = 1.0

def grid_speeds(count):
    spacing = 2.0 * speed_limit / count
    return -speed_limit + (jnp.arange(count, dtype=jnp.float32) + 0.5) * spacing

def upwind(padded, courant, along_dim, length):
    pieces = [lax.slice_in_dim(padded, offset, offset + length, axis=along_dim) for offset in range(5)]
    minus_two, minus_one, centre, plus_one, plus_two = pieces
    third = jnp.where(courant > 0, plus_one - 3.0 * centre + 3.0 * minus_one - minus_two, -(minus_one - 3.0 * centre + 3.0 * plus_one - plus_two))
    return centre - 0.5 * courant * (plus_one - minus_one) + 0.5 * courant * courant * (plus_one - 2.0 * centre + minus_one) - courant * (1.0 - courant * courant) / 6.0 * third

def moment_table(speeds_y, speeds_x, weight):
    along_y = speeds_y[:, None]
    along_x = speeds_x[None, :]
    square = along_x * along_x + along_y * along_y
    filler = jnp.ones_like(square)
    table = jnp.stack([filler, along_x * filler, along_y * filler, along_x * along_x * filler, along_x * along_y, along_y * along_y * filler, along_x * square, along_y * square])
    return table * weight

def moment_sums(table, swept):
    flat_table = table.reshape(table.shape[0], table.shape[1] * table.shape[2])
    flat_data = swept.reshape(swept.shape[0] * swept.shape[1], swept.shape[2] * swept.shape[3])
    result = jnp.dot(flat_table, flat_data, precision=lax.Precision.HIGHEST, preferred_element_type=jnp.float32)
    return result.reshape(table.shape[0], swept.shape[2], swept.shape[3])

def equilibrium_parts(sums):
    local_rho_value = sums[0]
    mean_flow_abscissa = sums[1] / local_rho_value
    mean_flow_ordinate = sums[2] / local_rho_value
    kinetic_content_sum = sums[3] + sums[5]
    lattice_norm_sq = mean_flow_abscissa * mean_flow_abscissa + mean_flow_ordinate * mean_flow_ordinate
    thermal_level = jnp.maximum(kinetic_content_sum / local_rho_value - lattice_norm_sq, thermal_floor)
    conduction_abscissa = 0.5 * (sums[6] - 2.0 * (mean_flow_abscissa * sums[3] + mean_flow_ordinate * sums[4]) - mean_flow_abscissa * kinetic_content_sum + 2.0 * local_rho_value * lattice_norm_sq * mean_flow_abscissa)
    conduction_ordinate = 0.5 * (sums[7] - 2.0 * (mean_flow_abscissa * sums[4] + mean_flow_ordinate * sums[5]) - mean_flow_ordinate * kinetic_content_sum + 2.0 * local_rho_value * lattice_norm_sq * mean_flow_ordinate)
    return (local_rho_value, mean_flow_abscissa, mean_flow_ordinate, thermal_level, conduction_abscissa, conduction_ordinate)

def relax(read, along_y, along_x, macroscopic_quantities):
    local_rho_value, mean_flow_abscissa, mean_flow_ordinate, thermal_level, conduction_abscissa, conduction_ordinate = macroscopic_quantities
    peculiar_abscissa = along_x - mean_flow_abscissa
    peculiar_ordinate = along_y - mean_flow_ordinate
    peculiar_norm_sq = peculiar_abscissa * peculiar_abscissa + peculiar_ordinate * peculiar_ordinate
    gaussian_equilibrium = local_rho_value / (math.pi * thermal_level) * jnp.exp(-peculiar_norm_sq / thermal_level)
    corrected_equilibrium = gaussian_equilibrium * (1.0 + 4.0 * (1.0 - viscous_conductive_ratio) * (conduction_abscissa * peculiar_abscissa + conduction_ordinate * peculiar_ordinate) / (local_rho_value * thermal_level * thermal_level) * (peculiar_norm_sq / thermal_level - 2.0))
    retain_mask = jnp.exp(-marching_delta * local_rho_value * jnp.sqrt(thermal_level) / inverse_relax_period)
    return corrected_equilibrium + (read - corrected_equilibrium) * retain_mask

def advance_once(current, speeds_y, speeds_x, table):
    rows = current.shape[2]
    cells = current.shape[3]
    wrapped = jnp.concatenate([current[:, :, :, cells - 2:], current, current[:, :, :, :2]], axis=3)
    swept = upwind(wrapped, marching_delta * speeds_x[None, :, None, None], 3, cells)
    mirrored = jnp.flip(swept, 0)
    lower = jnp.flip(mirrored[:, :, 0:2], 2)
    upper = jnp.flip(mirrored[:, :, rows - 2:rows], 2)
    walled = jnp.concatenate([lower, swept, upper], axis=2)
    swept = upwind(walled, marching_delta * speeds_y[:, None, None, None], 2, rows)
    sums = moment_sums(table, swept)
    macroscopic_quantities = equilibrium_parts(sums)
    return relax(swept, speeds_y[:, None, None, None], speeds_x[None, :, None, None], macroscopic_quantities)

def reference(populations):
    count_y = populations.shape[0]
    count_x = populations.shape[1]
    speeds_y = grid_speeds(count_y)
    speeds_x = grid_speeds(count_x)
    weight = 2.0 * speed_limit / count_y * (2.0 * speed_limit / count_x)
    table = moment_table(speeds_y, speeds_x, weight)
    current = populations
    for step_index in range(STEPS):
        current = advance_once(current, speeds_y, speeds_x, table)
    return current
```

```python
import math

import jax
import jax.numpy as jnp
from jax import lax
from jax.experimental import pallas as pl
from jax.experimental.pallas import tpu as pltpu
from jax.sharding import PartitionSpec as P

STEPS = 2
DT = 0.125
TAU0 = 16.0
PRANDTL = 2.0 / 3.0
FLOOR = 1.0
MESH = pl.DeviceIdType.MESH
F32 = jnp.float32

LY, LX, ROWS, CHUNKS, TILES = 2, 8, 32, 8, 4
LV = LY * LX
PAD = 48
CHIPS = 32


def speed(index):
    return (index.astype(F32) + 0.5) * 0.25 - 4.0


def taps(nu):
    a = jnp.abs(nu)
    e = a * (1.0 - a * a) * (1.0 / 6.0)
    h = 0.5 * a
    s = 0.5 * a * a
    return 1.0 - 2.0 * s + 3.0 * e, h + s - 3.0 * e, e, s - h - e


def total_wait(ref, sem):
    pltpu.make_async_copy(ref, ref, sem).wait()


def kernel(
    x_hbm, o_hbm, A, G, HS, HR, WS, WR, MO, R1, S, R2, T4, FO, FB,
    in_sem, out_sem, h_sem, w_sem, c_sem, rs_sem, ag_sem, d_sem,
):
    g, v, x = lax.axis_index("gx"), lax.axis_index("vy"), lax.axis_index("vx")
    z, yh, c = v // 4, (v // 2) % 2, v % 2
    other = 1 - c
    q_me = (x * 4 + z) * 2 + yh
    core_dev = (g, v + 1 - 2 * c, x)
    gx_dev = (1 - g, v, x)
    mirror_dev = (g, 15 - v, x)

    def chip(d):
        xx, zz, yy = (x + d // 8) % 4, (z + (d // 2) % 4) % 4, (yh + d % 2) % 2
        return (g, zz * 4 + yy * 2 + c, xx), (xx * 4 + zz) * 2 + yy

    barrier = pltpu.get_barrier_semaphore()

    def load(k):
        return pltpu.make_async_copy(
            x_hbm.at[:, :, pl.ds(k * 128, 128)], A.at[:, k], in_sem.at[k]
        )

    for k in range(CHUNKS):
        load(k).start()
    for d in (core_dev, gx_dev, mirror_dev):
        pl.semaphore_signal(barrier, inc=1, device_id=d, device_id_type=MESH)

    @pl.loop(1, CHIPS)
    def _(d):
        pl.semaphore_signal(barrier, inc=1, device_id=chip(d)[0], device_id_type=MESH)

    for k in range(CHUNKS):
        load(k).wait()
    pl.semaphore_wait(barrier, CHIPS - 1 + 3)

    lane = lax.broadcasted_iota(jnp.int32, (8, 128), 1)
    right = x >= 2
    up = v >= 8
    sx = jnp.where(right, 1, -1)
    kx0 = jnp.where(right, 0, 7)
    roll_u1 = jnp.where(right, 1, 127)
    roll_u2 = jnp.where(right, 2, 126)
    roll_d1 = jnp.where(right, 127, 1)
    edge = jnp.where(right, lane, 127 - lane)
    m_u1, m_u2, m_d1 = edge < 1, edge < 2, edge > 126
    sy = jnp.where(up, 1, -1)
    ghost0 = jnp.where(up, 0, 1)
    cx0 = x * LX
    cy = [speed(v * LY + j) for j in range(LY)]
    cy_taps = [taps(DT * s) for s in cy]
    mid = speed(cx0 + 3) + 0.125

    def step(n, _):
        HS[n] = jnp.zeros((2, 8, 128), F32)

        @pl.loop(0, LV)
        def _(ji):
            acc = jnp.zeros((8, 128), F32)
            for t in range(TILES):
                rows = pl.ds(8 * t, 8)
                head = pltpu.roll(A[ji, 0, rows, :], 4 * t, 1)
                tail = pltpu.roll(A[ji, 7, rows, :], (4 * t + 4) % 128, 1)
                acc = jnp.where((lane >= 4 * t) & (lane < 4 * t + 2), head, acc)
                acc = jnp.where((lane >= 4 * t + 2) & (lane < 4 * t + 4), tail, acc)
            HS[n, ji // 8] = HS[n, ji // 8] + pltpu.roll(acc, 16 * (ji % 8), 1)

        halo = pltpu.make_async_remote_copy(
            src_ref=HS.at[n], dst_ref=HR.at[n], send_sem=h_sem.at[n, 0], recv_sem=h_sem.at[n, 1],
            device_id=gx_dev, device_id_type=MESH,
        )
        halo.start()
        halo.wait()

        @pl.loop(0, LV * TILES)
        def _(it):
            ji, t = it // TILES, it % TILES
            rows = pl.ds(pl.multiple_of(8 * t, 8), 8)
            c0, c1, c2, c3 = taps(DT * speed(cx0 + ji % LX))
            ends = HR[n, ji // 8]
            base = 16 * (ji % 8) + 4 * t
            from_left = (252 - base) % 128
            from_right = (128 - base) % 128
            ext = [pltpu.roll(ends, jnp.where(right, from_left, from_right), 1)]
            where = [kx0 + sx * k for k in range(CHUNKS)]
            ext += [A[ji, k, rows, :] for k in where]
            ext += [pltpu.roll(ends, jnp.where(right, from_right, from_left), 1)]
            ru1 = [pltpu.roll(e, roll_u1, 1) for e in ext[:9]]
            ru2 = [pltpu.roll(e, roll_u2, 1) for e in ext[:9]]
            rd1 = [pltpu.roll(e, roll_d1, 1) for e in ext[1:]]
            for k in range(CHUNKS):
                u1 = jnp.where(m_u1, ru1[k], ru1[k + 1])
                u2 = jnp.where(m_u2, ru2[k], ru2[k + 1])
                d1 = jnp.where(m_d1, rd1[k + 1], rd1[k])
                out = (c0 * ext[k + 1] + c1 * u1) + (c2 * u2 + c3 * d1)
                G[ji, pl.ds(pl.multiple_of(where[k] * PAD + 8 + 8 * t, 8), 8), :] = out

        @pl.loop(0, 4 * LV)
        def _(it):
            r, ji = it // LV, it % LV
            row = jnp.where(r < 2, 1 - r, 33 - r) + 8
            WS[n, r, ji] = G[ji, pl.ds(row, 8, stride=PAD), :]

        send0 = 1 - ghost0
        mirror = pltpu.make_async_remote_copy(
            src_ref=WS.at[n, pl.ds(send0, 3)], dst_ref=WR.at[n, pl.ds(send0, 3)],
            send_sem=w_sem.at[n, 0], recv_sem=w_sem.at[n, 1],
            device_id=mirror_dev, device_id_type=MESH,
        )
        mirror.start()
        mirror.wait()

        @pl.loop(0, 3 * LV)
        def _(it):
            r, ji = it // LV + ghost0, it % LV
            row = jnp.where(r < 2, 6 + r, 38 + r)
            G[ji, pl.ds(row, 8, stride=PAD), :] = WR[n, r, (ji + 8) % 16]

        @pl.loop(0, TILES * CHUNKS)
        def _(it):
            t, k = it // CHUNKS, it % CHUNKS
            b = k * PAD + 8 + 8 * t
            rows = pl.ds(pl.multiple_of(8 * t, 8), 8)
            M = []
            for j in range(LY):
                c0, c1, c2, c3 = cy_taps[j]
                r = []
                for i in range(LX):
                    ji = j * LX + i
                    val = (
                        c0 * G[ji, pl.ds(b, 8), :] + c1 * G[ji, pl.ds(b - sy, 8), :]
                    ) + (c2 * G[ji, pl.ds(b - 2 * sy, 8), :] + c3 * G[ji, pl.ds(b + sy, 8), :])
                    A[ji, k, rows, :] = val
                    r.append(val)
                p = [r[4 + i] + r[3 - i] for i in range(4)]
                d = [r[4 + i] - r[3 - i] for i in range(4)]
                s = [0.125 + 0.25 * i for i in range(4)]
                L0 = (p[0] + p[1]) + (p[2] + p[3])
                L1 = (s[0] * d[0] + s[1] * d[1]) + (s[2] * d[2] + s[3] * d[3])
                L2 = (s[0] ** 2 * p[0] + s[1] ** 2 * p[1]) + (s[2] ** 2 * p[2] + s[3] ** 2 * p[3])
                L3 = (s[0] ** 3 * d[0] + s[1] ** 3 * d[1]) + (s[2] ** 3 * d[2] + s[3] ** 3 * d[3])
                M1 = L1 + mid * L0
                M2 = L2 + mid * (L1 + M1)
                M3 = L3 + mid * (3.0 * L2 + mid * (3.0 * L1 + mid * L0))
                M.append((L0, M1, M2, M3))
            (a0, a1, a2, a3), (b0, b1, b2, b3) = M
            ya, yb = cy
            ya0, yb0 = ya * a0, yb * b0
            ya1, yb1 = ya * a1, yb * b1
            sums = [
                a0 + b0,
                a1 + b1,
                ya0 + yb0,
                a2 + b2,
                ya1 + yb1,
                ya * ya0 + yb * yb0,
                (a3 + b3) + (ya * ya1 + yb * yb1),
                ya * (a2 + ya * ya0) + yb * (b2 + yb * yb0),
            ]
            for m in range(8):
                MO[n, k // 4, t, k % 4, pl.ds(m, 8, stride=8), :] = sums[m]

        core = pltpu.make_async_remote_copy(
            src_ref=MO.at[n, other], dst_ref=R1.at[n], send_sem=c_sem.at[n, 0], recv_sem=c_sem.at[n, 1],
            device_id=core_dev, device_id_type=MESH,
        )
        core.start()
        core.wait()

        @pl.loop(0, CHIPS)
        def _(q):
            rows = pl.ds(pl.multiple_of((q % 8) * 8, 8), 8)
            for t in range(TILES):
                S[n, q, t] = MO[n, c, t, q // 8, rows, :] + R1[n, t, q // 8, rows, :]

        @pl.loop(1, CHIPS)
        def _(d):
            dev, q = chip(d)
            pltpu.make_async_remote_copy(
                src_ref=S.at[n, q], dst_ref=R2.at[n, d - 1],
                send_sem=rs_sem.at[n, 0], recv_sem=rs_sem.at[n, 1],
                device_id=dev, device_id_type=MESH,
            ).start()

        total_wait(R2.at[n], rs_sem.at[n, 1])
        T4[...] = lax.fori_loop(
            0, CHIPS - 1, lambda d, acc: acc + R2[n, d], S[n, q_me], unroll=True
        ).reshape(TILES * 8, 128)
        s = [T4[pl.ds(m, TILES, stride=8), :] * 0.0625 for m in range(8)]
        rho = s[0]
        inv = 1.0 / rho
        ux, uy = s[1] * inv, s[2] * inv
        energy = s[3] + s[5]
        uu = ux * ux + uy * uy
        temp = jnp.maximum(energy * inv - uu, FLOOR)
        qx = 0.5 * (s[6] - 2.0 * (ux * s[3] + uy * s[4]) - ux * energy + 2.0 * rho * uu * ux)
        qy = 0.5 * (s[7] - 2.0 * (ux * s[4] + uy * s[5]) - uy * energy + 2.0 * rho * uu * uy)
        it = 1.0 / temp
        keep = jnp.exp((-DT / TAU0) * rho * jnp.sqrt(temp))
        scale = (4.0 * (1.0 - PRANDTL)) * inv * it * it
        fields = [ux, uy, it, rho * it * (1.0 / math.pi) * (1.0 - keep), keep, scale * qx, scale * qy, rho]
        for m in range(8):
            FO[n, pl.ds(m, TILES, stride=8), :] = fields[m]
        mine = FO[n]
        FB[n, c, pl.ds(pl.multiple_of(q_me * 32, 32), 32)] = mine

        @pl.loop(1, CHIPS)
        def _(d):
            dev, _q = chip(d)
            pltpu.make_async_remote_copy(
                src_ref=FO.at[n], dst_ref=FB.at[n, c, pl.ds(pl.multiple_of(q_me * 32, 32), 32)],
                send_sem=ag_sem.at[n, 0], recv_sem=ag_sem.at[n, 1],
                device_id=dev, device_id_type=MESH,
            ).start()

        total_wait(FB.at[n, c, pl.ds(0, (CHIPS - 1) * 32)], ag_sem.at[n, 1])
        back = pltpu.make_async_remote_copy(
            src_ref=FB.at[n, c], dst_ref=FB.at[n, c], send_sem=d_sem.at[n, 0], recv_sem=d_sem.at[n, 1],
            device_id=core_dev, device_id_type=MESH,
        )
        back.start()
        total_wait(R2.at[n], rs_sem.at[n, 0])
        total_wait(FB.at[n, c, pl.ds(0, (CHIPS - 1) * 32)], ag_sem.at[n, 0])
        back.wait()

        @pl.loop(0, TILES * CHUNKS)
        def _(it):
            t, k = it // CHUNKS, it % CHUNKS
            rows = pl.ds(pl.multiple_of(8 * t, 8), 8)
            first = (k % 4) * (8 * TILES * 8) + 8 * t
            ux, uy, it_, gp, keep, bx, by = [
                FB[n, k // 4, pl.ds(first + m, 8, stride=TILES * 8), :] for m in range(7)
            ]
            ax, ex, bxi = [], [], []
            for i in range(LX):
                xi = speed(cx0 + i) - ux
                a = xi * xi * it_
                ax.append(a)
                ex.append(jnp.exp(-a))
                bxi.append(bx * xi)
            for j in range(LY):
                yj = cy[j] - uy
                ay = yj * yj * it_
                ey = gp * jnp.exp(-ay)
                ay = ay - 2.0
                bj = by * yj
                for i in range(LX):
                    ji = j * LX + i
                    shakhov = ex[i] * ey * (1.0 + (bxi[i] + bj) * (ax[i] + ay))
                    A[ji, k, rows, :] = A[ji, k, rows, :] * keep + shakhov

        return 0

    lax.fori_loop(0, STEPS, step, 0)

    def store(k):
        return pltpu.make_async_copy(
            A.at[:, k], o_hbm.at[:, :, pl.ds(k * 128, 128)], out_sem.at[k]
        )

    for k in range(CHUNKS):
        store(k).start()
    for k in range(CHUNKS):
        store(k).wait()


def on_device(populations):
    shape = (LV, ROWS, CHUNKS * 128)
    dma = pltpu.SemaphoreType.DMA
    out = pl.pallas_call(
        kernel,
        out_shape=jax.ShapeDtypeStruct(shape, F32),
        in_specs=[pl.BlockSpec(memory_space=pl.ANY)],
        out_specs=pl.BlockSpec(memory_space=pl.ANY),
        scratch_shapes=[
            pltpu.VMEM((LV, CHUNKS, ROWS, 128), F32),
            pltpu.VMEM((LV, CHUNKS * PAD, 128), F32),
            pltpu.VMEM((STEPS, 2, 8, 128), F32),
            pltpu.VMEM((STEPS, 2, 8, 128), F32),
            pltpu.VMEM((STEPS, 4, LV, 8, 128), F32),
            pltpu.VMEM((STEPS, 4, LV, 8, 128), F32),
            pltpu.VMEM((STEPS, 2, TILES, 4, 64, 128), F32),
            pltpu.VMEM((STEPS, TILES, 4, 64, 128), F32),
            pltpu.VMEM((STEPS, CHIPS, TILES, 8, 128), F32),
            pltpu.VMEM((STEPS, CHIPS - 1, TILES, 8, 128), F32),
            pltpu.VMEM((TILES * 8, 128), F32),
            pltpu.VMEM((STEPS, TILES * 8, 128), F32),
            pltpu.VMEM((STEPS, 2, CHIPS * TILES * 8, 128), F32),
            dma((CHUNKS,)),
            dma((CHUNKS,)),
            dma((STEPS, 2)),
            dma((STEPS, 2)),
            dma((STEPS, 2)),
            dma((STEPS, 2)),
            dma((STEPS, 2)),
            dma((STEPS, 2)),
        ],
        compiler_params=pltpu.CompilerParams(
            collective_id=0, has_side_effects=True, vmem_limit_bytes=40 << 20
        ),
        cost_estimate=pl.CostEstimate(flops=60 << 20, bytes_accessed=4 << 20, transcendentals=1 << 20),
    )(populations.reshape(shape))
    return out.reshape(populations.shape)


def solution(mesh):
    return jax.shard_map(
        on_device,
        mesh=mesh,
        in_specs=(P("vy", "vx", None, "gx"),),
        out_specs=P("vy", "vx", None, "gx"),
        check_vma=False,
    )
```

```python
import math

import jax
import jax.numpy as jnp
from jax import lax
from jax.experimental import pallas as pl
from jax.experimental.pallas import tpu as pltpu
from jax.sharding import PartitionSpec as P

STEPS = 2
DT = 0.125
TAU0 = 16.0
PRANDTL = 2.0 / 3.0
FLOOR = 1.0
MESH = pl.DeviceIdType.MESH
F32 = jnp.float32

LY, LX, ROWS, CHUNKS, TILES = 2, 8, 32, 8, 4
LV = LY * LX
PAD = 48
CHIPS = 32
FAR_FIRST = sorted(
    ((a, b, e) for a in range(4) for b in range(4) for e in range(2) if a or b or e),
    key=lambda t: -(min(t[0], 4 - t[0]) + min(t[1], 4 - t[1]) + 2 * t[2]),
)


def speed(index):
    return (index.astype(F32) + 0.5) * 0.25 - 4.0


def taps(nu):
    a = jnp.abs(nu)
    e = a * (1.0 - a * a) * (1.0 / 6.0)
    h = 0.5 * a
    s = 0.5 * a * a
    return 1.0 - 2.0 * s + 3.0 * e, h + s - 3.0 * e, e, s - h - e


def total_wait(ref, sem):
    pltpu.make_async_copy(ref, ref, sem).wait()


def kernel(
    x_hbm, A, TX, G, HS, HR, HX, MO, R1, S, R2, T4, FO, FB,
    in_sem, h_sem, w_sem, c_sem, rs_sem, ag_sem, d_sem,
):
    g, v, x = lax.axis_index("gx"), lax.axis_index("vy"), lax.axis_index("vx")
    z, yh, c = v // 4, (v // 2) % 2, v % 2
    other = 1 - c
    q_me = (x * 4 + z) * 2 + yh
    core_dev = (g, v + 1 - 2 * c, x)
    gx_dev = (1 - g, v, x)
    mirror_dev = (g, 15 - v, x)
    chips = []
    for dx, dz, dy in FAR_FIRST:
        xx, zz, yy = (x + dx) % 4, (z + dz) % 4, (yh + dy) % 2
        chips.append(((g, zz * 4 + yy * 2 + c, xx), (xx * 4 + zz) * 2 + yy))

    load = pltpu.make_async_copy(x_hbm, A, in_sem)
    load.start()
    barrier = pltpu.get_barrier_semaphore()
    for d in (core_dev, gx_dev, mirror_dev):
        pl.semaphore_signal(barrier, inc=1, device_id=d, device_id_type=MESH)
    for d, _ in chips:
        pl.semaphore_signal(barrier, inc=1, device_id=d, device_id_type=MESH)

    cx0 = x * LX
    for i in range(LX):
        for m, tap in enumerate(taps(DT * speed(cx0 + i))):
            TX[i, m] = tap
    lane = lax.broadcasted_iota(jnp.int32, (8, 128), 1)
    right = x >= 2
    up = v >= 8
    sy = jnp.where(up, 1, -1)
    send0 = jnp.where(up, 1, 0)
    cy = [speed(v * LY + j) for j in range(LY)]
    cy_taps = [taps(DT * s) for s in cy]
    mid = speed(cx0 + 3) + 0.125

    load.wait()
    pl.semaphore_wait(barrier, CHIPS - 1 + 3)

    def tile(group, tt):
        return 1 + tt if group == 0 else 3 * tt

    def block(t, k):
        return pl.ds(pl.multiple_of(8 * t, 8), 8), pl.ds(pl.multiple_of(128 * k, 128), 128)

    def step(n, _):
        for part in range(2):
            acc = jnp.zeros((8, 128), F32)
            for p in range(32):
                ji, t = (part * 32 + p) // TILES, p % TILES
                ends = jnp.where(lane < 64, A[ji, 8 * t : 8 * t + 8, :128], A[ji, 8 * t : 8 * t + 8, 896:])
                ends = pltpu.roll(ends, (4 * p + 2) % 128, 1)
                acc = jnp.where((lane >= 4 * p) & (lane < 4 * p + 4), ends, acc)
            HS[n, part] = acc

        halo = pltpu.make_async_remote_copy(
            src_ref=HS.at[n], dst_ref=HR.at[n], send_sem=h_sem.at[n, 0], recv_sem=h_sem.at[n, 1],
            device_id=gx_dev, device_id_type=MESH,
        )
        halo.start()
        halo.wait()

        for part in range(2):
            ends = HR[n, part]
            for p in range(32):
                HX[part * 32 + p] = pltpu.roll(ends, (126 - 4 * p) % 128, 1)

        def stream(toward_right, tiles):
            order = list(range(CHUNKS)) if toward_right else list(range(CHUNKS - 1, -1, -1))
            edge = lane if toward_right else 127 - lane
            shift = (lambda a: a) if toward_right else (lambda a: 128 - a)
            m_u1, m_u2, m_d1 = edge < 1, edge < 2, edge > 126

            @pl.loop(0, LV)
            def _(ji):
                c0, c1, c2, c3 = [TX[ji % LX, m] for m in range(4)]
                for t in tiles:
                    ends = HX[ji * TILES + t]
                    ext = [ends] + [A[ji, 8 * t : 8 * t + 8, 128 * k : 128 * k + 128] for k in order] + [ends]
                    ru1 = [pltpu.roll(e, shift(1), 1) for e in ext[:9]]
                    ru2 = [pltpu.roll(e, shift(2), 1) for e in ext[:9]]
                    rd1 = [pltpu.roll(e, shift(127), 1) for e in ext[1:]]
                    for k in range(CHUNKS):
                        u1 = jnp.where(m_u1, ru1[k], ru1[k + 1])
                        u2 = jnp.where(m_u2, ru2[k], ru2[k + 1])
                        d1 = jnp.where(m_d1, rd1[k + 1], rd1[k])
                        out = (c0 * ext[k + 1] + c1 * u1) + (c2 * u2 + c3 * d1)
                        G[ji, order[k], pl.ds(8 + 8 * t, 8), :] = out

        def stream_tiles(*tiles):
            pl.when(right)(lambda: stream(True, tiles))
            pl.when(jnp.logical_not(right))(lambda: stream(False, tiles))

        stream_tiles(0, 3)

        mirrors = []
        for j in range(LY):
            for r in range(3):
                row = r + send0
                row = jnp.where(row < 2, 1 - row, 33 - row) + 8
                mirrors.append(pltpu.make_async_remote_copy(
                    src_ref=G.at[pl.ds(j * LX, LX), :, row, :],
                    dst_ref=G.at[pl.ds((1 - j) * LX, LX), :, jnp.where(row < 20, 15 - row, 79 - row), :],
                    send_sem=w_sem.at[n, 0, j * 3 + r], recv_sem=w_sem.at[n, 1, j * 3 + r],
                    device_id=mirror_dev, device_id_type=MESH,
                ))
        for m in mirrors:
            m.start()

        stream_tiles(1, 2)

        def sweep(group):
            @pl.loop(0, 2 * CHUNKS)
            def _(it):
                tt, k = it // CHUNKS, it % CHUNKS
                t = tile(group, tt)
                b = 8 + 8 * t
                rows, cols = block(t, k)
                M = []
                for j in range(LY):
                    c0, c1, c2, c3 = cy_taps[j]
                    r = []
                    for i in range(LX):
                        ji = j * LX + i
                        val = (
                            c0 * G[ji, k, pl.ds(b, 8), :] + c1 * G[ji, k, pl.ds(b - sy, 8), :]
                        ) + (c2 * G[ji, k, pl.ds(b - 2 * sy, 8), :] + c3 * G[ji, k, pl.ds(b + sy, 8), :])
                        A[ji, rows, cols] = val
                        r.append(val)
                    p = [r[4 + i] + r[3 - i] for i in range(4)]
                    d = [r[4 + i] - r[3 - i] for i in range(4)]
                    s = [0.125 + 0.25 * i for i in range(4)]
                    L0 = (p[0] + p[1]) + (p[2] + p[3])
                    L1 = (s[0] * d[0] + s[1] * d[1]) + (s[2] * d[2] + s[3] * d[3])
                    L2 = (s[0] ** 2 * p[0] + s[1] ** 2 * p[1]) + (s[2] ** 2 * p[2] + s[3] ** 2 * p[3])
                    L3 = (s[0] ** 3 * d[0] + s[1] ** 3 * d[1]) + (s[2] ** 3 * d[2] + s[3] ** 3 * d[3])
                    M1 = L1 + mid * L0
                    M2 = L2 + mid * (L1 + M1)
                    M3 = L3 + mid * (3.0 * L2 + mid * (3.0 * L1 + mid * L0))
                    M.append((L0, M1, M2, M3))
                (a0, a1, a2, a3), (b0, b1, b2, b3) = M
                ya, yb = cy
                ya0, yb0 = ya * a0, yb * b0
                ya1, yb1 = ya * a1, yb * b1
                sums = [
                    a0 + b0,
                    a1 + b1,
                    ya0 + yb0,
                    a2 + b2,
                    ya1 + yb1,
                    ya * ya0 + yb * yb0,
                    (a3 + b3) + (ya * ya1 + yb * yb1),
                    ya * (a2 + ya * ya0) + yb * (b2 + yb * yb0),
                ]
                for m in range(8):
                    MO[n, group, k // 4, tt, k % 4, pl.ds(m, 8, stride=8), :] = sums[m]

        def core_copy(group):
            return pltpu.make_async_remote_copy(
                src_ref=MO.at[n, group, other], dst_ref=R1.at[n, group],
                send_sem=c_sem.at[n, group, 0], recv_sem=c_sem.at[n, group, 1],
                device_id=core_dev, device_id_type=MESH,
            )

        def scatter(group):
            core_copy(group).wait()

            @pl.loop(0, 4)
            def _(kk):
                for r in range(8):
                    rows = pl.ds(8 * r, 8)
                    for tt in range(2):
                        S[n, group, kk * 8 + r, tt] = MO[n, group, c, tt, kk, rows, :] + R1[n, group, tt, kk, rows, :]

            for d, (dev, q) in enumerate(chips):
                pltpu.make_async_remote_copy(
                    src_ref=S.at[n, group, q], dst_ref=R2.at[n, group, d],
                    send_sem=rs_sem.at[n, group, 0], recv_sem=rs_sem.at[n, group, 1],
                    device_id=dev, device_id_type=MESH,
                ).start()

        def piece(q):
            return pl.ds(pl.multiple_of(q * 16, 16), 12)

        def gather(group):
            total_wait(R2.at[n, group], rs_sem.at[n, group, 1])
            parts = [S[n, group, q_me]] + [R2[n, group, d] for d in range(CHIPS - 1)]
            while len(parts) > 1:
                parts = [a + b for a, b in zip(parts[::2], parts[1::2])]
            T4[...] = parts[0].reshape(16, 128)
            s = [T4[pl.ds(m, 2, stride=8), :] * 0.0625 for m in range(8)]
            rho = s[0]
            inv = 1.0 / rho
            ux, uy = s[1] * inv, s[2] * inv
            energy = s[3] + s[5]
            uu = ux * ux + uy * uy
            temp = jnp.maximum(energy * inv - uu, FLOOR)
            qx = 0.5 * (s[6] - 2.0 * (ux * s[3] + uy * s[4]) - ux * energy + 2.0 * rho * uu * ux)
            qy = 0.5 * (s[7] - 2.0 * (ux * s[4] + uy * s[5]) - uy * energy + 2.0 * rho * uu * uy)
            cold = 1.0 / temp
            scale = (4.0 * (1.0 - PRANDTL)) * inv * cold * cold
            fields = jnp.concatenate([rho, ux, uy, cold, scale * qx, scale * qy], axis=0)
            FO[n, group] = fields
            FB[n, c, group, piece(q_me)] = fields
            for dev, _ in chips:
                pltpu.make_async_remote_copy(
                    src_ref=FO.at[n, group], dst_ref=FB.at[n, c, group, piece(q_me)],
                    send_sem=ag_sem.at[n, group, 0], recv_sem=ag_sem.at[n, group, 1],
                    device_id=dev, device_id_type=MESH,
                ).start()

        def back_copy(group):
            return pltpu.make_async_remote_copy(
                src_ref=FB.at[n, c, group], dst_ref=FB.at[n, c, group],
                send_sem=d_sem.at[n, group, 0], recv_sem=d_sem.at[n, group, 1],
                device_id=core_dev, device_id_type=MESH,
            )

        def all_pieces(group):
            return FB.at[n, c, group, pl.ds(0, (CHIPS - 1) * 12)]

        def relax(group):
            @pl.loop(0, 2 * CHUNKS)
            def _(it):
                tt, k = it // CHUNKS, it % CHUNKS
                rows, cols = block(tile(group, tt), k)
                first = (k % 4) * 128 + tt
                rho, ux, uy, cold, bx, by = [
                    FB[n, k // 4, group, pl.ds(first + 2 * m, 8, stride=16), :] for m in range(6)
                ]
                keep = jnp.exp((-DT / TAU0) * rho * lax.rsqrt(cold))
                gp = rho * cold * (1.0 / math.pi) * (1.0 - keep)
                ax, ex, bxi = [], [], []
                for i in range(LX):
                    xi = speed(cx0 + i) - ux
                    a = xi * xi * cold
                    ax.append(a)
                    ex.append(jnp.exp(-a))
                    bxi.append(bx * xi)
                for j in range(LY):
                    yj = cy[j] - uy
                    ay = yj * yj * cold
                    ey = gp * jnp.exp(-ay)
                    ay = ay - 2.0
                    bj = by * yj
                    for i in range(LX):
                        ji = j * LX + i
                        shakhov = ex[i] * ey * (1.0 + (bxi[i] + bj) * (ax[i] + ay))
                        A[ji, rows, cols] = A[ji, rows, cols] * keep + shakhov

        sweep(0)
        core_copy(0).start()
        scatter(0)
        for m in mirrors:
            m.wait()
        sweep(1)
        core_copy(1).start()
        scatter(1)
        gather(0)
        gather(1)
        for group in range(2):
            total_wait(all_pieces(group), ag_sem.at[n, group, 1])
            back_copy(group).start()
        for group in range(2):
            back_copy(group).wait()
            relax(group)
        for group in range(2):
            total_wait(R2.at[n, group], rs_sem.at[n, group, 0])
            total_wait(all_pieces(group), ag_sem.at[n, group, 0])
        return 0

    lax.fori_loop(0, STEPS, step, 0)


def on_device(populations):
    shape = (LV, ROWS, CHUNKS * 128)
    dma = pltpu.SemaphoreType.DMA
    out = pl.pallas_call(
        kernel,
        out_shape=pltpu.VMEM(shape, F32),
        in_specs=[pl.BlockSpec(memory_space=pltpu.HBM)],
        out_specs=pl.BlockSpec(memory_space=pltpu.VMEM),
        scratch_shapes=[
            pltpu.SMEM((LX, 4), F32),
            pltpu.VMEM((LV, CHUNKS, PAD, 128), F32),
            pltpu.VMEM((STEPS, 2, 8, 128), F32),
            pltpu.VMEM((STEPS, 2, 8, 128), F32),
            pltpu.VMEM((LV * TILES, 8, 128), F32),
            pltpu.VMEM((STEPS, 2, 2, 2, 4, 64, 128), F32),
            pltpu.VMEM((STEPS, 2, 2, 4, 64, 128), F32),
            pltpu.VMEM((STEPS, 2, CHIPS, 2, 8, 128), F32),
            pltpu.VMEM((STEPS, 2, CHIPS - 1, 2, 8, 128), F32),
            pltpu.VMEM((16, 128), F32),
            pltpu.VMEM((STEPS, 2, 12, 128), F32),
            pltpu.VMEM((STEPS, 2, 2, CHIPS * 16, 128), F32),
            dma,
            dma((STEPS, 2)),
            dma((STEPS, 2, 6)),
            dma((STEPS, 2, 2)),
            dma((STEPS, 2, 2)),
            dma((STEPS, 2, 2)),
            dma((STEPS, 2, 2)),
        ],
        compiler_params=pltpu.CompilerParams(
            collective_id=0, has_side_effects=True, vmem_limit_bytes=24 << 20
        ),
        cost_estimate=pl.CostEstimate(flops=60 << 20, bytes_accessed=4 << 20, transcendentals=1 << 20),
    )(populations.reshape(shape))
    return out.reshape(populations.shape)


def solution(mesh):
    return jax.shard_map(
        on_device,
        mesh=mesh,
        in_specs=(P("vy", "vx", None, "gx"),),
        out_specs=P("vy", "vx", None, "gx"),
        check_vma=False,
    )
```

```python
import math

import jax
import jax.numpy as jnp
from jax import lax
from jax.experimental import pallas as pl
from jax.experimental.pallas import tpu as pltpu
from jax.sharding import PartitionSpec as P

STEPS = 2
DT = 0.125
TAU0 = 16.0
PRANDTL = 2.0 / 3.0
FLOOR = 1.0
MESH = pl.DeviceIdType.MESH
F32 = jnp.float32

LY, LX, ROWS, CHUNKS, TILES = 2, 8, 32, 8, 4
LV = LY * LX
PAD = 48
CHIPS = 32
FAR_FIRST = sorted(
    ((a, b, e) for a in range(4) for b in range(4) for e in range(2) if a or b or e),
    key=lambda t: -(min(t[0], 4 - t[0]) + min(t[1], 4 - t[1]) + 2 * t[2]),
)


def speed(index):
    return (index.astype(F32) + 0.5) * 0.25 - 4.0


def taps(nu):
    a = jnp.abs(nu)
    e = a * (1.0 - a * a) * (1.0 / 6.0)
    h = 0.5 * a
    s = 0.5 * a * a
    return 1.0 - 2.0 * s + 3.0 * e, h + s - 3.0 * e, e, s - h - e


def total_wait(ref, sem):
    pltpu.make_async_copy(ref, ref, sem).wait()


def kernel(
    x_hbm, A, TX, G, GH, HS, HR, HX, MO, R1, S, R2, T4, FO, FB,
    in_sem, h_sem, w_sem, c_sem, rs_sem, ag_sem, d_sem,
):
    g, v, x = lax.axis_index("gx"), lax.axis_index("vy"), lax.axis_index("vx")
    z, yh, c = v // 4, (v // 2) % 2, v % 2
    other = 1 - c
    q_me = (x * 4 + z) * 2 + yh
    core_dev = (g, v + 1 - 2 * c, x)
    gx_dev = (1 - g, v, x)
    mirror_dev = (g, 15 - v, x)
    chips = []
    for dx, dz, dy in FAR_FIRST:
        xx, zz, yy = (x + dx) % 4, (z + dz) % 4, (yh + dy) % 2
        chips.append(((g, zz * 4 + yy * 2 + c, xx), (xx * 4 + zz) * 2 + yy))

    load = pltpu.make_async_copy(x_hbm, A, in_sem)
    load.start()
    @pl.loop(0, LV)
    def _(ji):
        for k in range(CHUNKS):
            G[ji, k, 0:8, :] = jnp.zeros((8, 128), F32)
            G[ji, k, 40:48, :] = jnp.zeros((8, 128), F32)
        for n in range(STEPS):
            for r in range(4):
                GH[n, r, ji] = jnp.zeros((8, 128), F32)

    barrier = pltpu.get_barrier_semaphore()
    for d in (core_dev, gx_dev, mirror_dev):
        pl.semaphore_signal(barrier, inc=1, device_id=d, device_id_type=MESH)
    for d, _ in chips:
        pl.semaphore_signal(barrier, inc=1, device_id=d, device_id_type=MESH)

    cx0 = x * LX
    for i in range(LX):
        for m, tap in enumerate(taps(DT * speed(cx0 + i))):
            TX[i, m] = tap
    lane = lax.broadcasted_iota(jnp.int32, (8, 128), 1)
    right = x >= 2
    up = v >= 8
    sy = jnp.where(up, 1, -1)
    sub = lax.broadcasted_iota(jnp.int32, (8, 128), 0)
    send0 = jnp.where(up, 1, 0)
    cy = [speed(v * LY + j) for j in range(LY)]
    cy_taps = [taps(DT * s) for s in cy]
    mid = speed(cx0 + 3) + 0.125

    pl.semaphore_wait(barrier, CHIPS - 1 + 3)

    load.wait()

    def rows_of(*pairs):
        out = jnp.zeros((8, 128), F32)
        for row, value in pairs:
            out = jnp.where(sub == row, value, out)
        return out

    reflect = []
    inward = []
    for j in range(LY):
        _, c1, c2, c3 = cy_taps[j]
        near, far = jnp.where(up, c3, c1), jnp.where(up, c1, c3)
        second, first = jnp.where(up, 0.0, c2), jnp.where(up, c2, 0.0)
        reflect.append((
            (rows_of((0, near)), rows_of((0, second)), rows_of((1, second))),
            (rows_of((7, far)), rows_of((6, first)), rows_of((7, first))),
        ))
        inward.append((
            (rows_of((0, first)), rows_of((0, far), (1, first))),
            (rows_of((7, near), (6, second)), rows_of((7, second))),
        ))

    def tile(group, tt):
        return 1 + tt if group == 0 else 3 * tt

    def block(t, k):
        return pl.ds(pl.multiple_of(8 * t, 8), 8), pl.ds(pl.multiple_of(128 * k, 128), 128)

    def step(n, _):
        halos = []
        for part in range(2):
            acc = jnp.zeros((8, 128), F32)
            for p in range(32):
                ji, t = (part * 32 + p) // TILES, p % TILES
                ends = jnp.where(lane < 64, A[ji, 8 * t : 8 * t + 8, :128], A[ji, 8 * t : 8 * t + 8, 896:])
                ends = pltpu.roll(ends, (4 * p + 2) % 128, 1)
                acc = jnp.where((lane >= 4 * p) & (lane < 4 * p + 4), ends, acc)
            HS[n, part] = acc
            halos.append(pltpu.make_async_remote_copy(
                src_ref=HS.at[n, part], dst_ref=HR.at[n, part],
                send_sem=h_sem.at[n, 0, part], recv_sem=h_sem.at[n, 1, part],
                device_id=gx_dev, device_id_type=MESH,
            ))
            halos[-1].start()

        def unpack():
            def place(toward_right):
                for part in range(2):
                    ends = HR[n, part]
                    for p in range(32):
                        for m, shift in enumerate((1, 2, 127) if toward_right else (127, 126, 1)):
                            HX[m, part * 32 + p] = pltpu.roll(ends, (126 - 4 * p + shift) % 128, 1)

            pl.when(right)(lambda: place(True))
            pl.when(jnp.logical_not(right))(lambda: place(False))

        def stream(toward_right, tiles, flow):
            edge = lane if toward_right else 127 - lane
            masks = (edge < 1, edge < 2, edge > 126)
            shifts = (1, 2, 127) if toward_right else (127, 126, 1)

            @pl.loop(0, LX)
            def _(i):
                c0, c1, c2, c3 = [TX[i, m] for m in range(4)]
                for j, t in [(j, t) for j in range(LY) for t in tiles]:
                    ji = j * LX + i
                    memo = {}

                    def chunk(f):
                        k = f if toward_right else CHUNKS - 1 - f
                        return A[ji, 8 * t : 8 * t + 8, 128 * k : 128 * k + 128]

                    def rolled(m, f):
                        if (m, f) not in memo:
                            if 0 <= f < CHUNKS:
                                memo[m, f] = pltpu.roll(chunk(f), shifts[m], 1)
                            else:
                                memo[m, f] = HX[m, ji * TILES + t]
                        return memo[m, f]

                    for f in flow:
                        u1 = jnp.where(masks[0], rolled(0, f - 1), rolled(0, f))
                        u2 = jnp.where(masks[1], rolled(1, f - 1), rolled(1, f))
                        d1 = jnp.where(masks[2], rolled(2, f + 1), rolled(2, f))
                        out = (c0 * chunk(f) + c1 * u1) + (c2 * u2 + c3 * d1)
                        k = f if toward_right else CHUNKS - 1 - f
                        G[ji, k, pl.ds(8 + 8 * t, 8), :] = out

        def stream_tiles(tiles, flow):
            pl.when(right)(lambda: stream(True, tiles, flow))
            pl.when(jnp.logical_not(right))(lambda: stream(False, tiles, flow))

        stream_tiles(range(TILES), range(1, CHUNKS - 1))
        for h in halos:
            h.wait()
        unpack()
        stream_tiles(range(TILES), (0, CHUNKS - 1))

        mirrors = []
        for j in range(LY):
            for r in range(3):
                e = r + send0
                row = jnp.where(e < 2, 1 - e, 33 - e) + 8
                mirrors.append(pltpu.make_async_remote_copy(
                    src_ref=G.at[pl.ds(j * LX, LX), :, row, :],
                    dst_ref=GH.at[n, e, pl.ds((1 - j) * LX, LX)],
                    send_sem=w_sem.at[n, 0, j * 3 + r], recv_sem=w_sem.at[n, 1, j * 3 + r],
                    device_id=mirror_dev, device_id_type=MESH,
                ))
        for m in mirrors:
            m.start()

        def add_ghosts():
            @pl.loop(0, LX)
            def _(i):
                for j in range(LY):
                    ji = j * LX + i
                    for tt in range(2):
                        wa, wb = inward[j][tt]
                        rows = slice(24 * tt, 24 * tt + 8)
                        for k in range(CHUNKS):
                            cols = slice(128 * k, 128 * k + 128)
                            A[ji, rows, cols] = A[ji, rows, cols] + (
                                wa * GH[n, 2 * tt, ji, pl.ds(k, 1), :] + wb * GH[n, 2 * tt + 1, ji, pl.ds(k, 1), :]
                            )

        def along_x(r):
            p = [r[4 + i] + r[3 - i] for i in range(4)]
            d = [r[4 + i] - r[3 - i] for i in range(4)]
            s = [0.125 + 0.25 * i for i in range(4)]
            L0 = (p[0] + p[1]) + (p[2] + p[3])
            L1 = (s[0] * d[0] + s[1] * d[1]) + (s[2] * d[2] + s[3] * d[3])
            L2 = (s[0] ** 2 * p[0] + s[1] ** 2 * p[1]) + (s[2] ** 2 * p[2] + s[3] ** 2 * p[3])
            L3 = (s[0] ** 3 * d[0] + s[1] ** 3 * d[1]) + (s[2] ** 3 * d[2] + s[3] ** 3 * d[3])
            M1 = L1 + mid * L0
            M2 = L2 + mid * (L1 + M1)
            M3 = L3 + mid * (3.0 * L2 + mid * (3.0 * L1 + mid * L0))
            return L0, M1, M2, M3

        def sweep(group):
            @pl.loop(0, CHUNKS)
            def _(k):
              for tt in range(2):
                t = tile(group, tt)
                b = 8 + 8 * t
                rows, cols = block(t, k)
                even, odd = [], []
                for j in range(LY):
                    c0, c1, c2, c3 = cy_taps[j]
                    r, centres = [], []
                    for i in range(LX):
                        ji = j * LX + i
                        centre = G[ji, k, pl.ds(b, 8), :]
                        val = (c0 * centre + c1 * G[ji, k, pl.ds(b - sy, 8), :]) + (
                            c2 * G[ji, k, pl.ds(b - 2 * sy, 8), :] + c3 * G[ji, k, pl.ds(b + sy, 8), :]
                        )
                        A[ji, rows, cols] = val
                        r.append(val)
                        centres.append(centre)
                    M = along_x(r)
                    if group == 0:
                        even.append(M)
                        odd.append(M)
                    else:
                        wa, wb, wc = reflect[j][tt]
                        X = [
                            (wa * m + wb * pltpu.roll(m, 7, 0)) + wc * pltpu.roll(m, 1, 0) for m in along_x(centres)
                        ]
                        even.append([m + e for m, e in zip(M, X)])
                        odd.append([m - e for m, e in zip(M, X)])
                (a0, a1, a2, a3), (b0, b1, b2, b3) = even
                (d0, d1, d2, _), (e0, e1, e2, _) = odd
                ya, yb = cy
                yya, yyb = ya * ya, yb * yb
                sums = [
                    a0 + b0,
                    a1 + b1,
                    ya * d0 + yb * e0,
                    a2 + b2,
                    ya * d1 + yb * e1,
                    yya * a0 + yyb * b0,
                    (a3 + b3) + (yya * a1 + yyb * b1),
                    ya * (d2 + yya * d0) + yb * (e2 + yyb * e0),
                ]
                for m in range(8):
                    MO[n, group, k // 4, tt, k % 4, pl.ds(m, 8, stride=8), :] = sums[m]

        def core_copy(group):
            return pltpu.make_async_remote_copy(
                src_ref=MO.at[n, group, other], dst_ref=R1.at[n, group],
                send_sem=c_sem.at[n, group, 0], recv_sem=c_sem.at[n, group, 1],
                device_id=core_dev, device_id_type=MESH,
            )

        def scatter(group):
            core_copy(group).wait()

            @pl.loop(0, 4)
            def _(kk):
                for r in range(8):
                    rows = pl.ds(8 * r, 8)
                    for tt in range(2):
                        S[n, group, kk * 8 + r, tt] = MO[n, group, c, tt, kk, rows, :] + R1[n, group, tt, kk, rows, :]

            for d, (dev, q) in enumerate(chips):
                pltpu.make_async_remote_copy(
                    src_ref=S.at[n, group, q], dst_ref=R2.at[n, group, d],
                    send_sem=rs_sem.at[n, group, 0], recv_sem=rs_sem.at[n, group, 1],
                    device_id=dev, device_id_type=MESH,
                ).start()

        def piece(q):
            return pl.ds(pl.multiple_of(q * 16, 16), 12)

        def gather(group):
            total_wait(R2.at[n, group], rs_sem.at[n, group, 1])
            parts = [S[n, group, q_me]] + [R2[n, group, d] for d in range(CHIPS - 1)]
            while len(parts) > 1:
                parts = [a + b for a, b in zip(parts[::2], parts[1::2])]
            T4[...] = parts[0].reshape(16, 128)
            s = [T4[pl.ds(m, 2, stride=8), :] * 0.0625 for m in range(8)]
            rho = s[0]
            inv = 1.0 / rho
            ux, uy = s[1] * inv, s[2] * inv
            energy = s[3] + s[5]
            uu = ux * ux + uy * uy
            temp = jnp.maximum(energy * inv - uu, FLOOR)
            qx = 0.5 * (s[6] - 2.0 * (ux * s[3] + uy * s[4]) - ux * energy + 2.0 * rho * uu * ux)
            qy = 0.5 * (s[7] - 2.0 * (ux * s[4] + uy * s[5]) - uy * energy + 2.0 * rho * uu * uy)
            cold = 1.0 / temp
            scale = (4.0 * (1.0 - PRANDTL)) * inv * cold * cold
            fields = jnp.concatenate([rho, ux, uy, cold, scale * qx, scale * qy], axis=0)
            FO[n, group] = fields
            FB[n, c, group, piece(q_me)] = fields
            for dev, _ in chips:
                pltpu.make_async_remote_copy(
                    src_ref=FO.at[n, group], dst_ref=FB.at[n, c, group, piece(q_me)],
                    send_sem=ag_sem.at[n, group, 0], recv_sem=ag_sem.at[n, group, 1],
                    device_id=dev, device_id_type=MESH,
                ).start()

        def back_copy(group):
            return pltpu.make_async_remote_copy(
                src_ref=FB.at[n, c, group], dst_ref=FB.at[n, c, group],
                send_sem=d_sem.at[n, group, 0], recv_sem=d_sem.at[n, group, 1],
                device_id=core_dev, device_id_type=MESH,
            )

        def all_pieces(group):
            return FB.at[n, c, group, pl.ds(0, (CHIPS - 1) * 12)]

        def relax(group):
            @pl.loop(0, CHUNKS)
            def _(k):
                first = (k % 4) * 128

                def one(values, speeds, at):
                    rho, ux, uy, cold, bx, by = values
                    keep = jnp.exp((-DT / TAU0) * rho * lax.rsqrt(cold))
                    gp = rho * cold * (1.0 / math.pi) * (1.0 - keep)
                    ax, ex, bxi = [], [], []
                    for i in range(LX):
                        xi = speed(cx0 + i) - ux
                        a = xi * xi * cold
                        ax.append(a)
                        ex.append(jnp.exp(-a))
                        bxi.append(bx * xi)
                    for j in range(LY):
                        yj = speeds[j] - uy
                        ay = yj * yj * cold
                        ey = gp * jnp.exp(-ay)
                        ay = ay - 2.0
                        bj = by * yj
                        for i in range(LX):
                            ref, rows, cols = at(j * LX + i)
                            shakhov = ex[i] * ey * (1.0 + (bxi[i] + bj) * (ax[i] + ay))
                            ref[rows, cols] = ref[rows, cols] * keep + shakhov

                fields = []
                for tt in range(2):
                    rows, cols = block(tile(group, tt), k)
                    fields.append([
                        FB[n, k // 4, group, pl.ds(first + tt + 2 * m, 8, stride=16), :] for m in range(6)
                    ])
                    one(fields[tt], cy, lambda ji: (A.at[ji], rows, cols))

        sweep(0)
        core_copy(0).start()
        sweep(1)
        core_copy(1).start()
        scatter(0)
        scatter(1)
        for m in mirrors:
            m.wait()
        add_ghosts()
        gather(0)
        gather(1)
        for group in range(2):
            total_wait(all_pieces(group), ag_sem.at[n, group, 1])
            back_copy(group).start()
        back_copy(0).wait()
        relax(0)

        back_copy(1).wait()
        relax(1)
        for group in range(2):
            total_wait(R2.at[n, group], rs_sem.at[n, group, 0])
            total_wait(all_pieces(group), ag_sem.at[n, group, 0])
        return 0

    lax.fori_loop(0, STEPS, step, 0)


def on_device(populations):
    shape = (LV, ROWS, CHUNKS * 128)
    dma = pltpu.SemaphoreType.DMA
    out = pl.pallas_call(
        kernel,
        out_shape=pltpu.VMEM(shape, F32),
        in_specs=[pl.BlockSpec(memory_space=pltpu.HBM)],
        out_specs=pl.BlockSpec(memory_space=pltpu.VMEM),
        scratch_shapes=[
            pltpu.SMEM((LX, 4), F32),
            pltpu.VMEM((LV, CHUNKS, PAD, 128), F32),
            pltpu.VMEM((STEPS, 4, LV, 8, 128), F32),
            pltpu.VMEM((STEPS, 2, 8, 128), F32),
            pltpu.VMEM((STEPS, 2, 8, 128), F32),
            pltpu.VMEM((3, LV * TILES, 8, 128), F32),
            pltpu.VMEM((STEPS, 2, 2, 2, 4, 64, 128), F32),
            pltpu.VMEM((STEPS, 2, 2, 4, 64, 128), F32),
            pltpu.VMEM((STEPS, 2, CHIPS, 2, 8, 128), F32),
            pltpu.VMEM((STEPS, 2, CHIPS - 1, 2, 8, 128), F32),
            pltpu.VMEM((16, 128), F32),
            pltpu.VMEM((STEPS, 2, 12, 128), F32),
            pltpu.VMEM((STEPS, 2, 2, CHIPS * 16, 128), F32),
            dma,
            dma((STEPS, 2, 2)),
            dma((STEPS, 2, 6)),
            dma((STEPS, 2, 2)),
            dma((STEPS, 2, 2)),
            dma((STEPS, 2, 2)),
            dma((STEPS, 2, 2)),
        ],
        compiler_params=pltpu.CompilerParams(
            collective_id=0, has_side_effects=True, vmem_limit_bytes=61 << 20
        ),
        cost_estimate=pl.CostEstimate(flops=60 << 20, bytes_accessed=4 << 20, transcendentals=1 << 20),
    )(populations.reshape(shape))
    return out.reshape(populations.shape)


def solution(mesh):
    return jax.shard_map(
        on_device,
        mesh=mesh,
        in_specs=(P("vy", "vx", None, "gx"),),
        out_specs=P("vy", "vx", None, "gx"),
        check_vma=False,
    )
```

```python
import math

import jax
import jax.numpy as jnp
from jax import lax
from jax.experimental import pallas as pl
from jax.experimental.pallas import tpu as pltpu
from jax.sharding import PartitionSpec as P

STEPS = 2
DT = 0.125
TAU0 = 16.0
PRANDTL = 2.0 / 3.0
FLOOR = 1.0
MESH = pl.DeviceIdType.MESH
F32 = jnp.float32

LY, LX, ROWS, CHUNKS, TILES = 2, 8, 32, 8, 4
LV = LY * LX
PAD = 48
CHIPS = 32
FAR_FIRST = sorted(
    ((a, b, e) for a in range(4) for b in range(4) for e in range(2) if a or b or e),
    key=lambda t: -(min(t[0], 4 - t[0]) + min(t[1], 4 - t[1]) + 2 * t[2]),
)


def speed(index):
    return (index.astype(F32) + 0.5) * 0.25 - 4.0


def taps(nu):
    a = jnp.abs(nu)
    e = a * (1.0 - a * a) * (1.0 / 6.0)
    h = 0.5 * a
    s = 0.5 * a * a
    return 1.0 - 2.0 * s + 3.0 * e, h + s - 3.0 * e, e, s - h - e


def total_wait(ref, sem):
    pltpu.make_async_copy(ref, ref, sem).wait()


def kernel(
    x_hbm, A, TX, G, GH, HS, HR, HX, MO, R1, S, R2, T4, FO, FB,
    in_sem, h_sem, w_sem, c_sem, rs_sem, ag_sem, d_sem,
):
    g, v, x = lax.axis_index("gx"), lax.axis_index("vy"), lax.axis_index("vx")
    z, yh, c = v // 4, (v // 2) % 2, v % 2
    other = 1 - c
    q_me = (x * 4 + z) * 2 + yh
    core_dev = (g, v + 1 - 2 * c, x)
    gx_dev = (1 - g, v, x)
    mirror_dev = (g, 15 - v, x)
    chips = []
    for dx, dz, dy in FAR_FIRST:
        xx, zz, yy = (x + dx) % 4, (z + dz) % 4, (yh + dy) % 2
        chips.append(((g, zz * 4 + yy * 2 + c, xx), (xx * 4 + zz) * 2 + yy))

    load = pltpu.make_async_copy(x_hbm, A, in_sem)
    load.start()
    @pl.loop(0, LV)
    def _(ji):
        for k in range(CHUNKS):
            G[ji, k, 0:8, :] = jnp.zeros((8, 128), F32)
            G[ji, k, 40:48, :] = jnp.zeros((8, 128), F32)
        for n in range(STEPS):
            for r in range(4):
                GH[n, r, ji] = jnp.zeros((8, 128), F32)

    barrier = pltpu.get_barrier_semaphore()
    for d in (core_dev, gx_dev, mirror_dev):
        pl.semaphore_signal(barrier, inc=1, device_id=d, device_id_type=MESH)
    for d, _ in chips:
        pl.semaphore_signal(barrier, inc=1, device_id=d, device_id_type=MESH)

    cx0 = x * LX
    for i in range(LX):
        for m, tap in enumerate(taps(DT * speed(cx0 + i))):
            TX[i, m] = tap
    lane = lax.broadcasted_iota(jnp.int32, (8, 128), 1)
    right = x >= 2
    up = v >= 8
    sy = jnp.where(up, 1, -1)
    sub = lax.broadcasted_iota(jnp.int32, (8, 128), 0)
    send0 = jnp.where(up, 1, 0)
    cy = [speed(v * LY + j) for j in range(LY)]
    cy_taps = [taps(DT * s) for s in cy]
    mid = speed(cx0 + 3) + 0.125

    pl.semaphore_wait(barrier, CHIPS - 1 + 3)

    load.wait()

    def rows_of(*pairs):
        out = jnp.zeros((8, 128), F32)
        for row, value in pairs:
            out = jnp.where(sub == row, value, out)
        return out

    reflect = []
    inward = []
    for j in range(LY):
        _, c1, c2, c3 = cy_taps[j]
        near, far = jnp.where(up, c3, c1), jnp.where(up, c1, c3)
        second, first = jnp.where(up, 0.0, c2), jnp.where(up, c2, 0.0)
        reflect.append((
            (rows_of((0, near)), rows_of((0, second)), rows_of((1, second))),
            (rows_of((7, far)), rows_of((6, first)), rows_of((7, first))),
        ))
        inward.append((
            (rows_of((0, first)), rows_of((0, far), (1, first))),
            (rows_of((7, near), (6, second)), rows_of((7, second))),
        ))

    def tile(group, tt):
        return 1 + tt if group == 0 else 3 * tt

    def block(t, k):
        return pl.ds(pl.multiple_of(8 * t, 8), 8), pl.ds(pl.multiple_of(128 * k, 128), 128)

    def step(n, _):
        halos = []
        for part in range(2):
            acc = jnp.zeros((8, 128), F32)
            for p in range(32):
                ji, t = (part * 32 + p) // TILES, p % TILES
                ends = jnp.where(lane < 64, A[ji, 8 * t : 8 * t + 8, :128], A[ji, 8 * t : 8 * t + 8, 896:])
                ends = pltpu.roll(ends, (4 * p + 2) % 128, 1)
                acc = jnp.where((lane >= 4 * p) & (lane < 4 * p + 4), ends, acc)
            HS[n, part] = acc
            halos.append(pltpu.make_async_remote_copy(
                src_ref=HS.at[n, part], dst_ref=HR.at[n, part],
                send_sem=h_sem.at[n, 0, part], recv_sem=h_sem.at[n, 1, part],
                device_id=gx_dev, device_id_type=MESH,
            ))
            halos[-1].start()

        def unpack():
            def place(toward_right):
                for part in range(2):
                    ends = HR[n, part]
                    for p in range(32):
                        for m, shift in enumerate((1, 2, 127) if toward_right else (127, 126, 1)):
                            HX[m, part * 32 + p] = pltpu.roll(ends, (126 - 4 * p + shift) % 128, 1)

            pl.when(right)(lambda: place(True))
            pl.when(jnp.logical_not(right))(lambda: place(False))

        def stream(toward_right, tiles, flow):
            edge = lane if toward_right else 127 - lane
            masks = (edge < 1, edge < 2, edge > 126)
            shifts = (1, 2, 127) if toward_right else (127, 126, 1)

            @pl.loop(0, LX)
            def _(i):
                c0, c1, c2, c3 = [TX[i, m] for m in range(4)]
                for j, t in [(j, t) for j in range(LY) for t in tiles]:
                    ji = j * LX + i
                    memo = {}

                    def chunk(f):
                        k = f if toward_right else CHUNKS - 1 - f
                        return A[ji, 8 * t : 8 * t + 8, 128 * k : 128 * k + 128]

                    def rolled(m, f):
                        if (m, f) not in memo:
                            if 0 <= f < CHUNKS:
                                memo[m, f] = pltpu.roll(chunk(f), shifts[m], 1)
                            else:
                                memo[m, f] = HX[m, ji * TILES + t]
                        return memo[m, f]

                    for f in flow:
                        u1 = jnp.where(masks[0], rolled(0, f - 1), rolled(0, f))
                        u2 = jnp.where(masks[1], rolled(1, f - 1), rolled(1, f))
                        d1 = jnp.where(masks[2], rolled(2, f + 1), rolled(2, f))
                        out = (c0 * chunk(f) + c1 * u1) + (c2 * u2 + c3 * d1)
                        k = f if toward_right else CHUNKS - 1 - f
                        G[ji, k, pl.ds(8 + 8 * t, 8), :] = out

        def stream_tiles(tiles, flow):
            pl.when(right)(lambda: stream(True, tiles, flow))
            pl.when(jnp.logical_not(right))(lambda: stream(False, tiles, flow))

        def mirror(part, first, count):
            copies = []
            for j in range(LY):
                for r in range(3):
                    e = r + send0
                    row = jnp.where(e < 2, 1 - e, 33 - e) + 8
                    copies.append(pltpu.make_async_remote_copy(
                        src_ref=G.at[pl.ds(j * LX, LX), pl.ds(first, count), row, :],
                        dst_ref=GH.at[n, e, pl.ds((1 - j) * LX, LX), pl.ds(first, count)],
                        send_sem=w_sem.at[n, 0, part * 6 + j * 3 + r], recv_sem=w_sem.at[n, 1, part * 6 + j * 3 + r],
                        device_id=mirror_dev, device_id_type=MESH,
                    ))
            for m in copies:
                m.start()
            return copies

        stream_tiles(range(TILES), range(1, CHUNKS - 1))
        mirrors = mirror(0, 1, CHUNKS - 2)
        for h in halos:
            h.wait()
        unpack()
        stream_tiles(range(TILES), (0, CHUNKS - 1))
        mirrors += mirror(1, 0, 1) + mirror(2, CHUNKS - 1, 1)

        def add_ghosts():
            @pl.loop(0, LX)
            def _(i):
                for j in range(LY):
                    ji = j * LX + i
                    for tt in range(2):
                        wa, wb = inward[j][tt]
                        rows = slice(24 * tt, 24 * tt + 8)
                        for k in range(CHUNKS):
                            cols = slice(128 * k, 128 * k + 128)
                            A[ji, rows, cols] = A[ji, rows, cols] + (
                                wa * GH[n, 2 * tt, ji, pl.ds(k, 1), :] + wb * GH[n, 2 * tt + 1, ji, pl.ds(k, 1), :]
                            )

        def along_x(r):
            p = [r[4 + i] + r[3 - i] for i in range(4)]
            d = [r[4 + i] - r[3 - i] for i in range(4)]
            s = [0.125 + 0.25 * i for i in range(4)]
            L0 = (p[0] + p[1]) + (p[2] + p[3])
            L1 = (s[0] * d[0] + s[1] * d[1]) + (s[2] * d[2] + s[3] * d[3])
            L2 = (s[0] ** 2 * p[0] + s[1] ** 2 * p[1]) + (s[2] ** 2 * p[2] + s[3] ** 2 * p[3])
            L3 = (s[0] ** 3 * d[0] + s[1] ** 3 * d[1]) + (s[2] ** 3 * d[2] + s[3] ** 3 * d[3])
            M1 = L1 + mid * L0
            M2 = L2 + mid * (L1 + M1)
            M3 = L3 + mid * (3.0 * L2 + mid * (3.0 * L1 + mid * L0))
            return L0, M1, M2, M3

        def sweep(group):
            @pl.loop(0, CHUNKS)
            def _(k):
              for tt in range(2):
                t = tile(group, tt)
                b = 8 + 8 * t
                rows, cols = block(t, k)
                even, odd = [], []
                for j in range(LY):
                    c0, c1, c2, c3 = cy_taps[j]
                    r, centres = [], []
                    for i in range(LX):
                        ji = j * LX + i
                        centre = G[ji, k, pl.ds(b, 8), :]
                        val = (c0 * centre + c1 * G[ji, k, pl.ds(b - sy, 8), :]) + (
                            c2 * G[ji, k, pl.ds(b - 2 * sy, 8), :] + c3 * G[ji, k, pl.ds(b + sy, 8), :]
                        )
                        A[ji, rows, cols] = val
                        r.append(val)
                        centres.append(centre)
                    M = along_x(r)
                    if group == 0:
                        even.append(M)
                        odd.append(M)
                    else:
                        wa, wb, wc = reflect[j][tt]
                        X = [
                            (wa * m + wb * pltpu.roll(m, 7, 0)) + wc * pltpu.roll(m, 1, 0) for m in along_x(centres)
                        ]
                        even.append([m + e for m, e in zip(M, X)])
                        odd.append([m - e for m, e in zip(M, X)])
                (a0, a1, a2, a3), (b0, b1, b2, b3) = even
                (d0, d1, d2, _), (e0, e1, e2, _) = odd
                ya, yb = cy
                yya, yyb = ya * ya, yb * yb
                sums = [
                    a0 + b0,
                    a1 + b1,
                    ya * d0 + yb * e0,
                    a2 + b2,
                    ya * d1 + yb * e1,
                    yya * a0 + yyb * b0,
                    (a3 + b3) + (yya * a1 + yyb * b1),
                    ya * (d2 + yya * d0) + yb * (e2 + yyb * e0),
                ]
                for m in range(8):
                    MO[n, group, k // 4, tt, k % 4, pl.ds(m, 8, stride=8), :] = sums[m]

        def core_copy(group):
            return pltpu.make_async_remote_copy(
                src_ref=MO.at[n, group, other], dst_ref=R1.at[n, group],
                send_sem=c_sem.at[n, group, 0], recv_sem=c_sem.at[n, group, 1],
                device_id=core_dev, device_id_type=MESH,
            )

        def scatter(group):
            core_copy(group).wait()

            @pl.loop(0, 4)
            def _(kk):
                for r in range(8):
                    rows = pl.ds(8 * r, 8)
                    for tt in range(2):
                        S[n, group, kk * 8 + r, tt] = MO[n, group, c, tt, kk, rows, :] + R1[n, group, tt, kk, rows, :]

            for d, (dev, q) in enumerate(chips):
                pltpu.make_async_remote_copy(
                    src_ref=S.at[n, group, q], dst_ref=R2.at[n, group, d],
                    send_sem=rs_sem.at[n, group, 0], recv_sem=rs_sem.at[n, group, 1],
                    device_id=dev, device_id_type=MESH,
                ).start()

        def piece(q):
            return pl.ds(pl.multiple_of(q * 16, 16), 12)

        def gather(group):
            total_wait(R2.at[n, group], rs_sem.at[n, group, 1])
            parts = [S[n, group, q_me]] + [R2[n, group, d] for d in range(CHIPS - 1)]
            while len(parts) > 1:
                parts = [a + b for a, b in zip(parts[::2], parts[1::2])]
            T4[...] = parts[0].reshape(16, 128)
            s = [T4[pl.ds(m, 2, stride=8), :] * 0.0625 for m in range(8)]
            rho = s[0]
            inv = 1.0 / rho
            ux, uy = s[1] * inv, s[2] * inv
            energy = s[3] + s[5]
            uu = ux * ux + uy * uy
            temp = jnp.maximum(energy * inv - uu, FLOOR)
            qx = 0.5 * (s[6] - 2.0 * (ux * s[3] + uy * s[4]) - ux * energy + 2.0 * rho * uu * ux)
            qy = 0.5 * (s[7] - 2.0 * (ux * s[4] + uy * s[5]) - uy * energy + 2.0 * rho * uu * uy)
            cold = 1.0 / temp
            scale = (4.0 * (1.0 - PRANDTL)) * inv * cold * cold
            fields = jnp.concatenate([rho, ux, uy, cold, scale * qx, scale * qy], axis=0)
            FO[n, group] = fields
            FB[n, c, group, piece(q_me)] = fields
            for dev, _ in chips:
                pltpu.make_async_remote_copy(
                    src_ref=FO.at[n, group], dst_ref=FB.at[n, c, group, piece(q_me)],
                    send_sem=ag_sem.at[n, group, 0], recv_sem=ag_sem.at[n, group, 1],
                    device_id=dev, device_id_type=MESH,
                ).start()

        def back_copy(group):
            return pltpu.make_async_remote_copy(
                src_ref=FB.at[n, c, group], dst_ref=FB.at[n, c, group],
                send_sem=d_sem.at[n, group, 0], recv_sem=d_sem.at[n, group, 1],
                device_id=core_dev, device_id_type=MESH,
            )

        def all_pieces(group):
            return FB.at[n, c, group, pl.ds(0, (CHIPS - 1) * 12)]

        def relax(group):
            @pl.loop(0, CHUNKS)
            def _(k):
                first = (k % 4) * 128

                def one(values, speeds, at):
                    rho, ux, uy, cold, bx, by = values
                    keep = jnp.exp((-DT / TAU0) * rho * lax.rsqrt(cold))
                    gp = rho * cold * (1.0 / math.pi) * (1.0 - keep)
                    ax, ex, bxi = [], [], []
                    for i in range(LX):
                        xi = speed(cx0 + i) - ux
                        a = xi * xi * cold
                        ax.append(a)
                        ex.append(jnp.exp(-a))
                        bxi.append(bx * xi)
                    for j in range(LY):
                        yj = speeds[j] - uy
                        ay = yj * yj * cold
                        ey = gp * jnp.exp(-ay)
                        ay = ay - 2.0
                        bj = by * yj
                        for i in range(LX):
                            ref, rows, cols = at(j * LX + i)
                            shakhov = ex[i] * ey * (1.0 + (bxi[i] + bj) * (ax[i] + ay))
                            ref[rows, cols] = ref[rows, cols] * keep + shakhov

                fields = []
                for tt in range(2):
                    rows, cols = block(tile(group, tt), k)
                    fields.append([
                        FB[n, k // 4, group, pl.ds(first + tt + 2 * m, 8, stride=16), :] for m in range(6)
                    ])
                    one(fields[tt], cy, lambda ji: (A.at[ji], rows, cols))

        sweep(0)
        core_copy(0).start()
        sweep(1)
        core_copy(1).start()
        scatter(0)
        scatter(1)
        for m in mirrors:
            m.wait()
        add_ghosts()
        gather(0)
        gather(1)
        for group in range(2):
            total_wait(all_pieces(group), ag_sem.at[n, group, 1])
            back_copy(group).start()
        back_copy(0).wait()
        relax(0)

        back_copy(1).wait()
        relax(1)
        for group in range(2):
            total_wait(R2.at[n, group], rs_sem.at[n, group, 0])
            total_wait(all_pieces(group), ag_sem.at[n, group, 0])
        return 0

    lax.fori_loop(0, STEPS, step, 0)


def on_device(populations):
    shape = (LV, ROWS, CHUNKS * 128)
    dma = pltpu.SemaphoreType.DMA
    out = pl.pallas_call(
        kernel,
        out_shape=pltpu.VMEM(shape, F32),
        in_specs=[pl.BlockSpec(memory_space=pltpu.HBM)],
        out_specs=pl.BlockSpec(memory_space=pltpu.VMEM),
        scratch_shapes=[
            pltpu.SMEM((LX, 4), F32),
            pltpu.VMEM((LV, CHUNKS, PAD, 128), F32),
            pltpu.VMEM((STEPS, 4, LV, 8, 128), F32),
            pltpu.VMEM((STEPS, 2, 8, 128), F32),
            pltpu.VMEM((STEPS, 2, 8, 128), F32),
            pltpu.VMEM((3, LV * TILES, 8, 128), F32),
            pltpu.VMEM((STEPS, 2, 2, 2, 4, 64, 128), F32),
            pltpu.VMEM((STEPS, 2, 2, 4, 64, 128), F32),
            pltpu.VMEM((STEPS, 2, CHIPS, 2, 8, 128), F32),
            pltpu.VMEM((STEPS, 2, CHIPS - 1, 2, 8, 128), F32),
            pltpu.VMEM((16, 128), F32),
            pltpu.VMEM((STEPS, 2, 12, 128), F32),
            pltpu.VMEM((STEPS, 2, 2, CHIPS * 16, 128), F32),
            dma,
            dma((STEPS, 2, 2)),
            dma((STEPS, 2, 18)),
            dma((STEPS, 2, 2)),
            dma((STEPS, 2, 2)),
            dma((STEPS, 2, 2)),
            dma((STEPS, 2, 2)),
        ],
        compiler_params=pltpu.CompilerParams(
            collective_id=0, has_side_effects=True, vmem_limit_bytes=61 << 20
        ),
        cost_estimate=pl.CostEstimate(flops=60 << 20, bytes_accessed=4 << 20, transcendentals=1 << 20),
    )(populations.reshape(shape))
    return out.reshape(populations.shape)


def solution(mesh):
    return jax.shard_map(
        on_device,
        mesh=mesh,
        in_specs=(P("vy", "vx", None, "gx"),),
        out_specs=P("vy", "vx", None, "gx"),
        check_vma=False,
    )
```

```python
import math

import jax
import jax.numpy as jnp
from jax import lax
from jax.experimental import pallas as pl
from jax.experimental.pallas import tpu as pltpu
from jax.sharding import PartitionSpec as P

STEPS = 2
DT = 0.125
TAU0 = 16.0
PRANDTL = 2.0 / 3.0
FLOOR = 1.0
MESH = pl.DeviceIdType.MESH
F32 = jnp.float32

LY, LX, ROWS, CHUNKS, TILES = 2, 8, 32, 8, 4
LV = LY * LX
PAD = 48
CHIPS = 32
FAR_FIRST = sorted(
    ((a, b, e) for a in range(4) for b in range(4) for e in range(2) if a or b or e),
    key=lambda t: -(min(t[0], 4 - t[0]) + min(t[1], 4 - t[1]) + 2 * t[2]),
)


def speed(index):
    return (index.astype(F32) + 0.5) * 0.25 - 4.0


def taps(nu):
    a = jnp.abs(nu)
    e = a * (1.0 - a * a) * (1.0 / 6.0)
    h = 0.5 * a
    s = 0.5 * a * a
    return 1.0 - 2.0 * s + 3.0 * e, h + s - 3.0 * e, e, s - h - e


def total_wait(ref, sem):
    pltpu.make_async_copy(ref, ref, sem).wait()


def kernel(
    x_hbm, A, TX, G, GH, HS, HR, HX, MO, R1, S, R2, T4, FO, FB,
    in_sem, h_sem, w_sem, c_sem, rs_sem, ag_sem, d_sem,
):
    g, v, x = lax.axis_index("gx"), lax.axis_index("vy"), lax.axis_index("vx")
    z, yh, c = v // 4, (v // 2) % 2, v % 2
    other = 1 - c
    q_me = (x * 4 + z) * 2 + yh
    core_dev = (g, v + 1 - 2 * c, x)
    gx_dev = (1 - g, v, x)
    mirror_dev = (g, 15 - v, x)
    chips = []
    for dx, dz, dy in FAR_FIRST:
        xx, zz, yy = (x + dx) % 4, (z + dz) % 4, (yh + dy) % 2
        chips.append(((g, zz * 4 + yy * 2 + c, xx), (xx * 4 + zz) * 2 + yy))

    load = pltpu.make_async_copy(x_hbm, A, in_sem)
    load.start()
    @pl.loop(0, LV)
    def _(ji):
        for k in range(CHUNKS):
            G[ji, k, 0:8, :] = jnp.zeros((8, 128), F32)
            G[ji, k, 40:48, :] = jnp.zeros((8, 128), F32)
        for n in range(STEPS):
            for r in range(4):
                GH[n, r, ji] = jnp.zeros((8, 128), F32)

    barrier = pltpu.get_barrier_semaphore()
    for d in (core_dev, gx_dev, mirror_dev):
        pl.semaphore_signal(barrier, inc=1, device_id=d, device_id_type=MESH)
    for d, _ in chips:
        pl.semaphore_signal(barrier, inc=1, device_id=d, device_id_type=MESH)

    cx0 = x * LX
    for i in range(LX):
        for m, tap in enumerate(taps(DT * speed(cx0 + i))):
            TX[i, m] = tap
    lane = lax.broadcasted_iota(jnp.int32, (8, 128), 1)
    right = x >= 2
    up = v >= 8
    sy = jnp.where(up, 1, -1)
    sub = lax.broadcasted_iota(jnp.int32, (8, 128), 0)
    send0 = jnp.where(up, 1, 0)
    cy = [speed(v * LY + j) for j in range(LY)]
    cy_taps = [taps(DT * s) for s in cy]
    mid = speed(cx0 + 3) + 0.125

    pl.semaphore_wait(barrier, CHIPS - 1 + 3)

    load.wait()

    def rows_of(*pairs):
        out = jnp.zeros((8, 128), F32)
        for row, value in pairs:
            out = jnp.where(sub == row, value, out)
        return out

    reflect = []
    inward = []
    for j in range(LY):
        _, c1, c2, c3 = cy_taps[j]
        near, far = jnp.where(up, c3, c1), jnp.where(up, c1, c3)
        second, first = jnp.where(up, 0.0, c2), jnp.where(up, c2, 0.0)
        reflect.append((
            (rows_of((0, near)), rows_of((0, second)), rows_of((1, second))),
            (rows_of((7, far)), rows_of((6, first)), rows_of((7, first))),
        ))
        inward.append((
            (rows_of((0, first)), rows_of((0, far), (1, first))),
            (rows_of((7, near), (6, second)), rows_of((7, second))),
        ))

    def tile(group, tt):
        return 1 + tt if group == 0 else 3 * tt

    def block(t, k):
        return pl.ds(pl.multiple_of(8 * t, 8), 8), pl.ds(pl.multiple_of(128 * k, 128), 128)

    def step(n, _):
        halos = []
        for part in range(2):
            acc = jnp.zeros((8, 128), F32)
            for p in range(32):
                ji, t = (part * 32 + p) // TILES, p % TILES
                ends = jnp.where(lane < 64, A[ji, 8 * t : 8 * t + 8, :128], A[ji, 8 * t : 8 * t + 8, 896:])
                ends = pltpu.roll(ends, (4 * p + 2) % 128, 1)
                acc = jnp.where((lane >= 4 * p) & (lane < 4 * p + 4), ends, acc)
            HS[n, part] = acc
            halos.append(pltpu.make_async_remote_copy(
                src_ref=HS.at[n, part], dst_ref=HR.at[n, part],
                send_sem=h_sem.at[n, 0, part], recv_sem=h_sem.at[n, 1, part],
                device_id=gx_dev, device_id_type=MESH,
            ))
            halos[-1].start()

        def unpack():
            def place(toward_right):
                for part in range(2):
                    ends = HR[n, part]
                    for p in range(32):
                        for m, shift in enumerate((1, 2, 127) if toward_right else (127, 126, 1)):
                            HX[m, part * 32 + p] = pltpu.roll(ends, (126 - 4 * p + shift) % 128, 1)

            pl.when(right)(lambda: place(True))
            pl.when(jnp.logical_not(right))(lambda: place(False))

        def stream(toward_right, tiles, flow):
            edge = lane if toward_right else 127 - lane
            masks = (edge < 1, edge < 2, edge > 126)
            shifts = (1, 2, 127) if toward_right else (127, 126, 1)

            @pl.loop(0, LX)
            def _(i):
                c0, c1, c2, c3 = [TX[i, m] for m in range(4)]
                for j, t in [(j, t) for j in range(LY) for t in tiles]:
                    ji = j * LX + i
                    memo = {}

                    def chunk(f):
                        k = f if toward_right else CHUNKS - 1 - f
                        return A[ji, 8 * t : 8 * t + 8, 128 * k : 128 * k + 128]

                    def rolled(m, f):
                        if (m, f) not in memo:
                            if 0 <= f < CHUNKS:
                                memo[m, f] = pltpu.roll(chunk(f), shifts[m], 1)
                            else:
                                memo[m, f] = HX[m, ji * TILES + t]
                        return memo[m, f]

                    for f in flow:
                        u1 = jnp.where(masks[0], rolled(0, f - 1), rolled(0, f))
                        u2 = jnp.where(masks[1], rolled(1, f - 1), rolled(1, f))
                        d1 = jnp.where(masks[2], rolled(2, f + 1), rolled(2, f))
                        out = (c0 * chunk(f) + c1 * u1) + (c2 * u2 + c3 * d1)
                        k = f if toward_right else CHUNKS - 1 - f
                        G[ji, k, pl.ds(8 + 8 * t, 8), :] = out

        def stream_tiles(tiles, flow):
            pl.when(right)(lambda: stream(True, tiles, flow))
            pl.when(jnp.logical_not(right))(lambda: stream(False, tiles, flow))

        def mirror(part, first, count):
            copies = []
            for j in range(LY):
                for r in range(3):
                    e = r + send0
                    row = jnp.where(e < 2, 1 - e, 33 - e) + 8
                    copies.append(pltpu.make_async_remote_copy(
                        src_ref=G.at[pl.ds(j * LX, LX), pl.ds(first, count), row, :],
                        dst_ref=GH.at[n, e, pl.ds((1 - j) * LX, LX), pl.ds(first, count)],
                        send_sem=w_sem.at[n, 0, part * 6 + j * 3 + r], recv_sem=w_sem.at[n, 1, part * 6 + j * 3 + r],
                        device_id=mirror_dev, device_id_type=MESH,
                    ))
            for m in copies:
                m.start()
            return copies

        stream_tiles((0, 3), range(1, CHUNKS - 1))
        mirrors = mirror(0, 1, CHUNKS - 2)
        stream_tiles((1, 2), range(1, CHUNKS - 1))
        for h in halos:
            h.wait()
        unpack()
        stream_tiles((0, 3), (0, CHUNKS - 1))
        mirrors += mirror(1, 0, 1) + mirror(2, CHUNKS - 1, 1)
        stream_tiles((1, 2), (0, CHUNKS - 1))

        def add_ghosts():
            @pl.loop(0, LX)
            def _(i):
                for j in range(LY):
                    ji = j * LX + i
                    for tt in range(2):
                        wa, wb = inward[j][tt]
                        rows = slice(24 * tt, 24 * tt + 8)
                        for k in range(CHUNKS):
                            cols = slice(128 * k, 128 * k + 128)
                            A[ji, rows, cols] = A[ji, rows, cols] + (
                                wa * GH[n, 2 * tt, ji, pl.ds(k, 1), :] + wb * GH[n, 2 * tt + 1, ji, pl.ds(k, 1), :]
                            )

        def along_x(r):
            p = [r[4 + i] + r[3 - i] for i in range(4)]
            d = [r[4 + i] - r[3 - i] for i in range(4)]
            s = [0.125 + 0.25 * i for i in range(4)]
            L0 = (p[0] + p[1]) + (p[2] + p[3])
            L1 = (s[0] * d[0] + s[1] * d[1]) + (s[2] * d[2] + s[3] * d[3])
            L2 = (s[0] ** 2 * p[0] + s[1] ** 2 * p[1]) + (s[2] ** 2 * p[2] + s[3] ** 2 * p[3])
            L3 = (s[0] ** 3 * d[0] + s[1] ** 3 * d[1]) + (s[2] ** 3 * d[2] + s[3] ** 3 * d[3])
            M1 = L1 + mid * L0
            M2 = L2 + mid * (L1 + M1)
            M3 = L3 + mid * (3.0 * L2 + mid * (3.0 * L1 + mid * L0))
            return L0, M1, M2, M3

        def sweep(group):
            @pl.loop(0, CHUNKS)
            def _(k):
              for tt in range(2):
                t = tile(group, tt)
                b = 8 + 8 * t
                rows, cols = block(t, k)
                even, odd = [], []
                for j in range(LY):
                    c0, c1, c2, c3 = cy_taps[j]
                    r, centres = [], []
                    for i in range(LX):
                        ji = j * LX + i
                        centre = G[ji, k, pl.ds(b, 8), :]
                        val = (c0 * centre + c1 * G[ji, k, pl.ds(b - sy, 8), :]) + (
                            c2 * G[ji, k, pl.ds(b - 2 * sy, 8), :] + c3 * G[ji, k, pl.ds(b + sy, 8), :]
                        )
                        A[ji, rows, cols] = val
                        r.append(val)
                        centres.append(centre)
                    M = along_x(r)
                    if group == 0:
                        even.append(M)
                        odd.append(M)
                    else:
                        wa, wb, wc = reflect[j][tt]
                        X = [
                            (wa * m + wb * pltpu.roll(m, 7, 0)) + wc * pltpu.roll(m, 1, 0) for m in along_x(centres)
                        ]
                        even.append([m + e for m, e in zip(M, X)])
                        odd.append([m - e for m, e in zip(M, X)])
                (a0, a1, a2, a3), (b0, b1, b2, b3) = even
                (d0, d1, d2, _), (e0, e1, e2, _) = odd
                ya, yb = cy
                yya, yyb = ya * ya, yb * yb
                sums = [
                    a0 + b0,
                    a1 + b1,
                    ya * d0 + yb * e0,
                    a2 + b2,
                    ya * d1 + yb * e1,
                    yya * a0 + yyb * b0,
                    (a3 + b3) + (yya * a1 + yyb * b1),
                    ya * (d2 + yya * d0) + yb * (e2 + yyb * e0),
                ]
                for m in range(8):
                    MO[n, group, k // 4, tt, k % 4, pl.ds(m, 8, stride=8), :] = sums[m]

        def core_copy(group):
            return pltpu.make_async_remote_copy(
                src_ref=MO.at[n, group, other], dst_ref=R1.at[n, group],
                send_sem=c_sem.at[n, group, 0], recv_sem=c_sem.at[n, group, 1],
                device_id=core_dev, device_id_type=MESH,
            )

        def scatter(group):
            core_copy(group).wait()

            @pl.loop(0, 4)
            def _(kk):
                for r in range(8):
                    rows = pl.ds(8 * r, 8)
                    for tt in range(2):
                        S[n, group, kk * 8 + r, tt] = MO[n, group, c, tt, kk, rows, :] + R1[n, group, tt, kk, rows, :]

            for d, (dev, q) in enumerate(chips):
                pltpu.make_async_remote_copy(
                    src_ref=S.at[n, group, q], dst_ref=R2.at[n, group, d],
                    send_sem=rs_sem.at[n, group, 0], recv_sem=rs_sem.at[n, group, 1],
                    device_id=dev, device_id_type=MESH,
                ).start()

        def piece(q):
            return pl.ds(pl.multiple_of(q * 16, 16), 12)

        def gather(group):
            total_wait(R2.at[n, group], rs_sem.at[n, group, 1])
            parts = [S[n, group, q_me]] + [R2[n, group, d] for d in range(CHIPS - 1)]
            while len(parts) > 1:
                parts = [a + b for a, b in zip(parts[::2], parts[1::2])]
            T4[...] = parts[0].reshape(16, 128)
            s = [T4[pl.ds(m, 2, stride=8), :] * 0.0625 for m in range(8)]
            rho = s[0]
            inv = 1.0 / rho
            ux, uy = s[1] * inv, s[2] * inv
            energy = s[3] + s[5]
            uu = ux * ux + uy * uy
            temp = jnp.maximum(energy * inv - uu, FLOOR)
            qx = 0.5 * (s[6] - 2.0 * (ux * s[3] + uy * s[4]) - ux * energy + 2.0 * rho * uu * ux)
            qy = 0.5 * (s[7] - 2.0 * (ux * s[4] + uy * s[5]) - uy * energy + 2.0 * rho * uu * uy)
            cold = 1.0 / temp
            scale = (4.0 * (1.0 - PRANDTL)) * inv * cold * cold
            fields = jnp.concatenate([rho, ux, uy, cold, scale * qx, scale * qy], axis=0)
            FO[n, group] = fields
            FB[n, c, group, piece(q_me)] = fields
            for dev, _ in chips:
                pltpu.make_async_remote_copy(
                    src_ref=FO.at[n, group], dst_ref=FB.at[n, c, group, piece(q_me)],
                    send_sem=ag_sem.at[n, group, 0], recv_sem=ag_sem.at[n, group, 1],
                    device_id=dev, device_id_type=MESH,
                ).start()

        def back_copy(group):
            return pltpu.make_async_remote_copy(
                src_ref=FB.at[n, c, group], dst_ref=FB.at[n, c, group],
                send_sem=d_sem.at[n, group, 0], recv_sem=d_sem.at[n, group, 1],
                device_id=core_dev, device_id_type=MESH,
            )

        def all_pieces(group):
            return FB.at[n, c, group, pl.ds(0, (CHIPS - 1) * 12)]

        def relax(group):
            @pl.loop(0, CHUNKS)
            def _(k):
                first = (k % 4) * 128

                def one(values, speeds, at):
                    rho, ux, uy, cold, bx, by = values
                    keep = jnp.exp((-DT / TAU0) * rho * lax.rsqrt(cold))
                    gp = rho * cold * (1.0 / math.pi) * (1.0 - keep)
                    ax, ex, bxi = [], [], []
                    for i in range(LX):
                        xi = speed(cx0 + i) - ux
                        a = xi * xi * cold
                        ax.append(a)
                        ex.append(jnp.exp(-a))
                        bxi.append(bx * xi)
                    for j in range(LY):
                        yj = speeds[j] - uy
                        ay = yj * yj * cold
                        ey = gp * jnp.exp(-ay)
                        ay = ay - 2.0
                        bj = by * yj
                        for i in range(LX):
                            ref, rows, cols = at(j * LX + i)
                            shakhov = ex[i] * ey * (1.0 + (bxi[i] + bj) * (ax[i] + ay))
                            ref[rows, cols] = ref[rows, cols] * keep + shakhov

                fields = []
                for tt in range(2):
                    rows, cols = block(tile(group, tt), k)
                    fields.append([
                        FB[n, k // 4, group, pl.ds(first + tt + 2 * m, 8, stride=16), :] for m in range(6)
                    ])
                    one(fields[tt], cy, lambda ji: (A.at[ji], rows, cols))

        sweep(0)
        core_copy(0).start()
        sweep(1)
        core_copy(1).start()
        scatter(0)
        scatter(1)
        for m in mirrors:
            m.wait()
        add_ghosts()
        gather(0)
        gather(1)
        for group in range(2):
            total_wait(all_pieces(group), ag_sem.at[n, group, 1])
            back_copy(group).start()
        back_copy(0).wait()
        relax(0)

        back_copy(1).wait()
        relax(1)
        for group in range(2):
            total_wait(R2.at[n, group], rs_sem.at[n, group, 0])
            total_wait(all_pieces(group), ag_sem.at[n, group, 0])
        return 0

    lax.fori_loop(0, STEPS, step, 0)


def on_device(populations):
    shape = (LV, ROWS, CHUNKS * 128)
    dma = pltpu.SemaphoreType.DMA
    out = pl.pallas_call(
        kernel,
        out_shape=pltpu.VMEM(shape, F32),
        in_specs=[pl.BlockSpec(memory_space=pltpu.HBM)],
        out_specs=pl.BlockSpec(memory_space=pltpu.VMEM),
        scratch_shapes=[
            pltpu.SMEM((LX, 4), F32),
            pltpu.VMEM((LV, CHUNKS, PAD, 128), F32),
            pltpu.VMEM((STEPS, 4, LV, 8, 128), F32),
            pltpu.VMEM((STEPS, 2, 8, 128), F32),
            pltpu.VMEM((STEPS, 2, 8, 128), F32),
            pltpu.VMEM((3, LV * TILES, 8, 128), F32),
            pltpu.VMEM((STEPS, 2, 2, 2, 4, 64, 128), F32),
            pltpu.VMEM((STEPS, 2, 2, 4, 64, 128), F32),
            pltpu.VMEM((STEPS, 2, CHIPS, 2, 8, 128), F32),
            pltpu.VMEM((STEPS, 2, CHIPS - 1, 2, 8, 128), F32),
            pltpu.VMEM((16, 128), F32),
            pltpu.VMEM((STEPS, 2, 12, 128), F32),
            pltpu.VMEM((STEPS, 2, 2, CHIPS * 16, 128), F32),
            dma,
            dma((STEPS, 2, 2)),
            dma((STEPS, 2, 18)),
            dma((STEPS, 2, 2)),
            dma((STEPS, 2, 2)),
            dma((STEPS, 2, 2)),
            dma((STEPS, 2, 2)),
        ],
        compiler_params=pltpu.CompilerParams(
            collective_id=0, has_side_effects=True, vmem_limit_bytes=61 << 20
        ),
        cost_estimate=pl.CostEstimate(flops=60 << 20, bytes_accessed=4 << 20, transcendentals=1 << 20),
    )(populations.reshape(shape))
    return out.reshape(populations.shape)


def solution(mesh):
    return jax.shard_map(
        on_device,
        mesh=mesh,
        in_specs=(P("vy", "vx", None, "gx"),),
        out_specs=P("vy", "vx", None, "gx"),
        check_vma=False,
    )
```
